32 devices in a mesh: groups: 2 (over y), loop: 16 (over z, x, core).
Axes of the slice: x: 2, y: 2, z: 4, core: 2. Of those that a mesh axis runs over, the one named last changes fastest.
Arguments:
- store: bfloat16 [384, 9216], P(('groups', 'loop')), parts along dimension 0
- source: int32 [384], P(('groups', 'loop')), parts along dimension 0, may hold values from 0 to 191, each once
- lengths: int32 [12], P('groups'), parts along dimension 0, may hold values from 1 to 96, 192 in all
- block_table: int32 [72], P('groups'), parts along dimension 0, may hold values from 0 to 35, each once
- ln_gain: float32 [9216], replicated, may hold values from 0.1 to 1.9
- ln_bias: float32 [9216], replicated, may hold values from -3 to 3
- kv_weight: bfloat16 [9216, 16384], P(None, 'loop'), may hold values from -0.0625 to 0.0625
- kv_bias: float32 [16384], P('loop'), may hold values from -3 to 3
- cache: bfloat16 [72, 16, 16384], P('groups', None, 'loop'), parts along dimension 0, may hold values from -6 to 6
Outputs:
- cache_out: bfloat16 [72, 16, 16384], P('groups', None, 'loop'), parts along dimension 0
The draws below stay inside these ranges and needn't reach their ends.
There are 2 independent parts, one for each index of `groups`. The reference program is written for one: setup_inputs(seed, part) draws one part's arguments, and reference() takes and returns one part's arrays. A program takes and returns all parts, laid end to end along the dimension named above; an argument that names none is the same for every part. Nothing has to cross between parts.
Inputs may be any that keep to these rules, and one draw needn't show every extreme that they name: source is a permutation of the store rows.
All inputs are finite; a program needn't handle non-finite values.
Results may differ from the reference program's by a relative error of at most 0.0029.
Values may be sent and summed in bfloat16 or wider, within the bound.
A program may use at most 192 MiB of HBM per device.

```python
import math
import jax
import jax.numpy as jnp
import numpy as np
from jax import lax

D = 9216
PAGE = 16
SESS = 6
KVW = 16384
TOKENS = 192
MOSTLEN = 96
PAGES = 36


def draw_store(key, part):
    key = jax.random.fold_in(key, 3)
    first, second = jax.random.split(key, 2)
    scale = jnp.exp(jax.random.uniform(second, (TOKENS, 1), minval=0.0, maxval=math.log(10.0)))
    values = jax.random.normal(first, (TOKENS, D)) * scale
    return values.astype(jnp.bfloat16)


def steps_of(own_key, extent, cuts, least, high):
    level, own = 1.0, jax.random.fold_in(own_key, 6)
    for dim, parts in cuts:
        heights = jnp.exp(jax.random.uniform(jax.random.fold_in(own, dim), (parts,), jnp.float32, least / len(cuts), high / len(cuts)))
        level = level * jnp.repeat(heights, extent[dim] // parts).reshape([-1 if axis == dim else 1 for axis in range(len(extent))])
    return level


def length_profile(count, total, most, skew):
    loads = [(1 << 20) // math.isqrt(rank ** skew) + 1 for rank in range(2, count + 1)]
    spare, holding = total - most - (count - 1), [1] * (count - 1)
    while spare > 0:
        candidates = [i for i in range(count - 1) if holding[i] < most]
        whole, left = sum([loads[i] for i in candidates]), spare
        for i in candidates:
            addition = min(most - holding[i], max(1, left * loads[i] // whole), spare)
            holding[i] = holding[i] + addition
            spare = spare - addition
    return np.array([most] + holding)


def uneven(key, count, total, most, skew):
    if count == 2:
        one = jax.random.randint(key, (), max(1, total - most), min(most, total - 1) + 1)
        return jnp.stack([one, total - one])
    sizes = jnp.asarray(length_profile(count, total, most, skew), jnp.int32)
    pairs = (count - 1) // 2
    donor, sink = sizes[1:1 + 2 * pairs:2], sizes[2:2 + 2 * pairs:2]
    margin = jnp.minimum(donor - 1, most - sink)
    moved = jax.random.randint(jax.random.fold_in(key, 1), (pairs,), 0, 1 << 20) % (margin + 1)
    sizes = sizes.at[1:1 + 2 * pairs:2].set(donor - moved).at[2:2 + 2 * pairs:2].set(sink + moved)
    return sizes[jax.random.permutation(jax.random.fold_in(key, 2), count)]


def centred(stream_key, shape, scale, most, cuts=(), kind=jnp.bfloat16):
    gain = steps_of(stream_key, shape, cuts, -0.22, 0.18) if cuts else 1.0
    entries = jax.random.normal(stream_key, shape, jnp.float32) * scale * gain
    return jnp.minimum(jnp.maximum(entries, -most), most).astype(kind)


def setup_inputs(seed: int = 0, part: int = 0) -> dict:
    keys = jax.random.split(jax.random.key(seed), 10)
    own_keys = jax.random.split(jax.random.fold_in(keys[9], part), 10)
    store = draw_store(jax.random.fold_in(jax.random.fold_in(keys[9], part), 71), part)
    source = jax.random.permutation(own_keys[1], TOKENS).astype(jnp.int32)
    lengths = uneven(own_keys[2], SESS, TOKENS, MOSTLEN, 2).astype(jnp.int32)
    block_table = jax.random.permutation(own_keys[3], PAGES).astype(jnp.int32)
    ln_gain = jnp.clip(1.0 + 0.18 * jax.random.normal(keys[4], (D,), jnp.float32), 0.1, 1.9)
    ln_bias = centred(keys[5], (D,), 0.5, 3.0, (), jnp.float32)
    kv_weight = centred(keys[6], (D, KVW), D ** -0.5, 0.0625, ((1, 16),))
    kv_bias = centred(keys[7], (KVW,), 0.5, 3.0, ((0, 16),), jnp.float32)
    cache = centred(own_keys[8], (PAGES, PAGE, KVW), 1.0, 6.0, ((2, 16),))
    return {"store": store, "source": source, "lengths": lengths, "block_table": block_table, "ln_gain": ln_gain, "ln_bias": ln_bias, "kv_weight": kv_weight, "kv_bias": kv_bias, "cache": cache}


def layer_norm(rows, ln_gain, ln_bias):
    values = rows.astype(jnp.float32)
    center = values - lax.optimization_barrier(jnp.mean(values, axis=-1, keepdims=True))
    spread = lax.optimization_barrier(jnp.mean(center * center, axis=-1, keepdims=True))
    return (center * lax.rsqrt(spread + 1e-05) * ln_gain + ln_bias).astype(jnp.bfloat16)

def cache_rows(lengths, block_table, total):
    ends = jnp.cumsum(lengths).astype(jnp.int32)
    token = jnp.arange(total, dtype=jnp.int32)
    passed = (token[:, None] >= ends[None, :]).astype(jnp.int32)
    session = lax.optimization_barrier(jnp.sum(passed, axis=1)).astype(jnp.int32)
    position = (token - lax.optimization_barrier(jnp.sum(passed * lengths[None, :], axis=1))).astype(jnp.int32)
    per_session = block_table.shape[0] // lengths.shape[0]
    entry = (session * per_session + position // PAGE).astype(jnp.int32)
    table_ids = jnp.arange(block_table.shape[0], dtype=jnp.int32)
    page = lax.optimization_barrier(jnp.sum(jnp.where(table_ids[None, :] == entry[:, None], block_table[None, :], 0), axis=1))
    return (page * PAGE + position % PAGE).astype(jnp.int32)

def reference(store, source, lengths, block_table, ln_gain, ln_bias, kv_weight, kv_bias, cache):
    restored = jnp.take(store, source, axis=0)
    normed = layer_norm(restored, ln_gain, ln_bias)
    new_rows = (jnp.dot(normed, kv_weight, preferred_element_type=jnp.float32) + kv_bias).astype(jnp.bfloat16)
    dest = cache_rows(lengths, block_table, TOKENS)
    flat = cache.reshape(PAGES * PAGE, cache.shape[2])
    return flat.at[dest].set(new_rows).reshape(cache.shape)
```

```python
import jax
import jax.numpy as jnp
from jax import lax
from jax.experimental import pallas as pl
from jax.experimental.pallas import tpu as pltpu
from jax.sharding import PartitionSpec as P

PAGE = 16


def layer_norm(rows, ln_gain, ln_bias):
    values = rows.astype(jnp.float32)
    center = values - jnp.mean(values, axis=-1, keepdims=True)
    spread = jnp.mean(center * center, axis=-1, keepdims=True)
    return (center * lax.rsqrt(spread + 1e-05) * ln_gain + ln_bias).astype(jnp.bfloat16)


def cache_rows(lengths, block_table, total):
    ends = jnp.cumsum(lengths)
    token = jnp.arange(total, dtype=jnp.int32)
    passed = (token[:, None] >= ends[None, :]).astype(jnp.int32)
    session = jnp.sum(passed, axis=1)
    position = token - jnp.sum(passed * lengths[None, :], axis=1)
    per_session = block_table.shape[0] // lengths.shape[0]
    entry = session * per_session + position // PAGE
    table_ids = jnp.arange(block_table.shape[0], dtype=jnp.int32)
    page = jnp.sum(jnp.where(table_ids[None, :] == entry[:, None], block_table[None, :], 0), axis=1)
    return page * PAGE + position % PAGE


SEGS = 6
RING = 8
MESH = pl.DeviceIdType.MESH


def kernel(
    store, source, lengths, table, gain, bias, weight, kv_bias, cache, out,
    normed, packed, rows, held, extra, total, every, spread, pages, meta,
    to_right, to_left, to_twin, from_ring, from_twin,
    meta_right, meta_left, meta_twin, meta_ring, meta_from_twin,
    weight_sem, cache_sem, out_sem,
):
    count, width = store.shape
    main = width * 3 // 4
    seg_width, third = main // SEGS, width // 4
    half = SEGS // 2
    features = kv_bias.shape[1]
    slots = 2 * RING * 16
    pages_rows = pages.shape[0]

    me = lax.axis_index("loop")
    core, chip = lax.rem(me, 2), me // 2
    side = RING // 2
    place = chip // 2 + lax.rem(chip, 2) * (RING - 1 - 2 * (chip // 2))

    def device(step, which):
        at = lax.rem(place + step + RING, RING)
        column = at // side
        line = at + column * (RING - 1 - 2 * at)
        return 2 * (2 * line + column) + which

    right, left, twin = device(1, core), device(-1, core), device(0, 1 - core)

    parts = weight_sem.shape[0]
    depth = width // parts

    def weight_copy(i):
        span = pl.ds(pl.multiple_of(i * depth, depth), depth)
        return pltpu.make_async_copy(weight.at[span], held.at[span], weight_sem.at[i])

    barrier = pltpu.get_barrier_semaphore()
    for other in (right, left, twin):
        pl.semaphore_signal(barrier, inc=1, device_id={"loop": other}, device_id_type=MESH)
    for i in range(parts):
        weight_copy(i).start()
    cache_copy = pltpu.make_async_copy(cache, pages, cache_sem)
    cache_copy.start()

    values = store[...].astype(jnp.float32)
    center = values - jnp.mean(values, axis=-1, keepdims=True)
    var = jnp.mean(center * center, axis=-1, keepdims=True)
    normed[0:count, :] = center * lax.rsqrt(var + 1e-05) * gain[...] + bias[...]
    packed[0:count, :] = normed[0:count, 0:main]
    for s in range(3):
        packed[12:16, s * third:(s + 1) * third] = normed[4 * s:4 * s + 4, main:width]

    def row(m, which):
        return pl.multiple_of((2 * m + which) * 16, 16)

    rows[pl.ds(row(0, core), 16), :] = packed[...].astype(jnp.bfloat16)

    line = lax.broadcasted_iota(jnp.int32, (16, 128), 0)
    marks = jnp.full((16, 128), -1, jnp.int32)
    for i in range(count):
        marks = jnp.where(line == i, source[i], marks)

    def meta_at(dev):
        return meta.at[pl.ds(pl.multiple_of(dev * 16, 16), 16)]

    meta[pl.ds(pl.multiple_of(me * 16, 16), 16), :] = marks.astype(jnp.float32).astype(jnp.bfloat16)

    def block(m, seg):
        return rows.at[pl.ds(row(m, core), 16), pl.ds(pl.multiple_of(seg * seg_width, 128), seg_width)]

    def remote(src, dst, send, recv, dev):
        return pltpu.make_async_remote_copy(
            src_ref=src, dst_ref=dst, send_sem=send, recv_sem=recv,
            device_id={"loop": dev}, device_id_type=MESH,
        )

    def right_copy(k, seg):
        return remote(
            block(2 * k - 1 if k else 0, seg), block(2 * k + 1, seg),
            to_right.at[k, seg], from_ring.at[0, k, seg], right,
        )

    def left_copy(k, seg):
        return remote(
            block(2 * k, seg), block(2 * k + 2 if k < 3 else 7, seg),
            to_left.at[k, seg], from_ring.at[1, k, seg], left,
        )

    def twin_copy(m, seg):
        return remote(block(m, seg), block(m, seg), to_twin.at[m, seg], from_twin.at[m, seg], twin)

    def meta_copy(way, k, owner):
        sends = (meta_right, meta_left)[way]
        ref = meta_at(device(owner, core))
        return remote(ref, ref, sends.at[k], meta_ring.at[way, k], (right, left)[way])

    def meta_twin_copy(m, owner, which):
        ref = meta_at(device(owner, which))
        return remote(ref, ref, meta_twin.at[m], meta_from_twin.at[m], twin)

    pl.semaphore_wait(barrier, 3)

    @pl.loop(0, SEGS)
    def _(seg):
        right_copy(0, seg).start()
        left_copy(0, seg).start()
        twin_copy(0, seg).start()

    meta_copy(0, 0, 0).start()
    meta_copy(1, 0, 0).start()
    meta_twin_copy(0, 0, core).start()

    total[...] = jnp.zeros_like(total)
    extra[...] = jnp.zeros_like(extra)

    def multiply(base, size, seg):
        cols = pl.ds(pl.multiple_of(seg * seg_width, 128), seg_width)
        deep = pl.ds(pl.multiple_of(seg * seg_width, seg_width), seg_width)
        total[base:base + size, :] += jnp.dot(
            rows[base:base + size, cols], held[deep, :], preferred_element_type=jnp.float32
        )

    def finish(base, size, owners):
        for b in range(size // 16):
            for s in range(3):
                piece = rows[base + 16 * b:base + 16 * b + 16, s * third:(s + 1) * third]
                extra[16 * b + 4 * s:16 * b + 4 * s + 4, :] = piece.astype(jnp.float32)[12:16]
        result = total[base:base + size, :] + jnp.dot(
            extra[0:size, :].astype(jnp.bfloat16), held[main:width, :],
            preferred_element_type=jnp.float32,
        )
        result = (result + kv_bias[...]).astype(jnp.bfloat16)
        for b in range(size // 16):
            dev = device(owners[b // 2], b % 2)
            every[pl.ds(pl.multiple_of(dev * 16, 16), 16), :] = result[16 * b:16 * b + 16]

    def group(k):
        if k == 0:
            return (0,), 0, 32, (0,)
        if k == 4:
            return (7,), 224, 32, (-4,)
        return (2 * k - 1, 2 * k), (2 * k - 1) * 32, 64, (-k, k)

    def work(k, seg):
        members, base, size, _ = group(k)
        for m in members:
            twin_copy(m, seg).wait_recv()
        if k == 0:
            weight_copy(seg).wait()
        multiply(base, size, seg)

    for k in range(1, 4):
        @pl.loop(0, SEGS)
        def _(seg, k=k):
            right_copy(k - 1, seg).wait_recv()
            if k < 3:
                right_copy(k, seg).start()
            else:
                @pl.when(seg < half)
                def _():
                    right_copy(k, seg).start()
            twin_copy(2 * k - 1, seg).start()
            left_copy(k - 1, seg).wait_recv()
            if k < 3:
                left_copy(k, seg).start()
            else:
                @pl.when(seg >= half)
                def _():
                    left_copy(k, seg).start()
            twin_copy(2 * k, seg).start()
            work(k - 1, seg)

        meta_copy(0, k - 1, -k).wait_recv()
        meta_copy(0, k, -k).start()
        meta_twin_copy(2 * k - 1, -k, core).start()
        meta_copy(1, k - 1, k).wait_recv()
        if k < 3:
            meta_copy(1, k, k).start()
        meta_twin_copy(2 * k, k, core).start()
        if k == 1:
            for i in range(SEGS, parts):
                weight_copy(i).wait()
        _, base, size, owners = group(k - 1)
        finish(base, size, owners)

    meta_copy(0, 3, -4).wait_recv()
    meta_twin_copy(7, -4, core).start()

    @pl.loop(0, half)
    def _(j):
        right_copy(3, j).wait_recv()
        twin_copy(7, j).start()
        left_copy(3, j + half).wait_recv()
        twin_copy(7, j + half).start()
        work(3, 2 * j)
        work(3, 2 * j + 1)

    _, base, size, owners = group(3)
    finish(base, size, owners)

    for m, owner in ((0, 0), (1, -1), (2, 1), (3, -2), (4, 2), (5, -3), (6, 3), (7, -4)):
        meta_twin_copy(m, owner, 1 - core).wait_recv()
    slot = lax.broadcasted_iota(jnp.int32, (1, slots), 1)
    index = (slot // 16) * count + lax.rem(slot, 16)
    real = lax.rem(slot, 16) < count
    wanted = jnp.where(real, index, -2).astype(jnp.float32)
    asked = meta[...].astype(jnp.float32)
    asked = jnp.concatenate([asked] * (slots // 128), axis=1)
    pick = jnp.where(asked == wanted, 1.0, 0.0).astype(jnp.bfloat16)
    sessions, entries = lengths.shape[0], table.shape[0]
    session = jnp.zeros_like(index)
    position = index
    end = jnp.int32(0)
    for s in range(sessions):
        end = end + lengths[s]
        passed = index >= end
        session = session + jnp.where(passed, 1, 0)
        position = position - jnp.where(passed, lengths[s], 0)
    entry = session * (entries // sessions) + lax.shift_right_logical(position, 4)
    page = jnp.zeros_like(index)
    for e in range(entries):
        page = jnp.where(entry == e, table[e], page)
    dest = jnp.where(real, page * PAGE + jnp.bitwise_and(position, PAGE - 1), -1)
    where = lax.broadcasted_iota(jnp.int32, (pages_rows, slots), 0)
    put = jnp.where(where == dest, 1.0, 0.0).astype(jnp.bfloat16)
    spread[...] = jnp.dot(put, pick, preferred_element_type=jnp.float32).astype(jnp.bfloat16)
    cache_copy.wait()

    @pl.loop(0, half)
    def _(j):
        work(4, j)
        work(4, j + half)

    _, base, size, owners = group(4)
    finish(base, size, owners)

    chunks = out_sem.shape[0]
    high = pages_rows // chunks

    def out_copy(i):
        span = pl.ds(pl.multiple_of(i * high, 16), high)
        return pltpu.make_async_copy(pages.at[span], out.at[span], out_sem.at[i])

    @pl.loop(0, chunks)
    def _(i):
        span = pl.ds(pl.multiple_of(i * high, 16), high)
        choice = spread[span, :]
        new = jnp.dot(choice, every[...], preferred_element_type=jnp.float32)
        taken = jnp.sum(choice.astype(jnp.float32), axis=1, keepdims=True) > 0.5
        pages[span, :] = jnp.where(taken, new, pages[span, :].astype(jnp.float32)).astype(jnp.bfloat16)
        out_copy(i).start()

    for k in range(4):
        @pl.loop(0, half if k == 3 else SEGS)
        def _(seg, k=k):
            right_copy(k, seg).wait_send()
            left_copy(k, seg + half if k == 3 else seg).wait_send()
        meta_copy(0, k, -k).wait_send()
        if k < 3:
            meta_copy(1, k, k).wait_send()
    for m, owner in ((0, 0), (1, -1), (2, 1), (3, -2), (4, 2), (5, -3), (6, 3), (7, -4)):
        meta_twin_copy(m, owner, core).wait_send()

        @pl.loop(0, SEGS)
        def _(seg, m=m):
            twin_copy(m, seg).wait_send()

    @pl.loop(0, chunks)
    def _(i):
        out_copy(i).wait()


def fused(store, source, lengths, table, ln_gain, ln_bias, kv_weight, kv_bias, cache):
    count, width = store.shape
    features = kv_weight.shape[1]
    pages_rows = cache.shape[0] * cache.shape[1]
    slots = 2 * RING * 16
    parts, chunks = 8, 6
    vmem, smem, hbm = (
        pl.BlockSpec(memory_space=pltpu.VMEM),
        pl.BlockSpec(memory_space=pltpu.SMEM),
        pl.BlockSpec(memory_space=pltpu.HBM),
    )
    dma = pltpu.SemaphoreType.DMA
    result = pl.pallas_call(
        kernel,
        out_shape=jax.ShapeDtypeStruct((pages_rows, features), jnp.bfloat16),
        in_specs=[vmem, smem, smem, smem, vmem, vmem, hbm, vmem, hbm],
        out_specs=hbm,
        scratch_shapes=[
            pltpu.VMEM((16, width), jnp.float32),
            pltpu.VMEM((16, width * 3 // 4), jnp.float32),
            pltpu.VMEM((slots, width * 3 // 4), jnp.bfloat16),
            pltpu.VMEM((width, features), jnp.bfloat16),
            pltpu.VMEM((64, width // 4), jnp.float32),
            pltpu.VMEM((slots, features), jnp.float32),
            pltpu.VMEM((slots, features), jnp.bfloat16),
            pltpu.VMEM((pages_rows, slots), jnp.bfloat16),
            pltpu.VMEM((pages_rows, features), jnp.bfloat16),
            pltpu.VMEM((slots, 128), jnp.bfloat16),
            dma((4, SEGS)), dma((4, SEGS)), dma((8, SEGS)), dma((2, 4, SEGS)), dma((8, SEGS)),
            dma((4,)), dma((4,)), dma((8,)), dma((2, 4)), dma((8,)),
            dma((parts,)), dma, dma((chunks,)),
        ],
        compiler_params=pltpu.CompilerParams(
            collective_id=0, has_side_effects=True, vmem_limit_bytes=56 * 1024 * 1024
        ),
        cost_estimate=pl.CostEstimate(
            flops=2 * slots * width * features, transcendentals=0,
            bytes_accessed=2 * width * features + 4 * pages_rows * features,
        ),
    )(
        store, source, lengths, table, ln_gain.reshape(1, width), ln_bias.reshape(1, width),
        kv_weight, kv_bias.reshape(1, features), cache.reshape(pages_rows, features),
    )
    return result.reshape(cache.shape)


def local(store, source, lengths, block_table, ln_gain, ln_bias, kv_weight, kv_bias, cache):
    rows_dev = store.shape[0]
    devices = lax.axis_size("loop")
    total = rows_dev * devices
    if devices == 2 * RING and rows_dev == 12:
        return fused(store, source, lengths, block_table, ln_gain, ln_bias, kv_weight, kv_bias, cache)
    every_source = lax.all_gather(source, "loop", axis=0, tiled=True)
    product = jnp.dot(
        lax.all_gather(layer_norm(store, ln_gain, ln_bias), "loop", axis=0, tiled=True),
        kv_weight,
        preferred_element_type=jnp.float32,
    )
    by_slot = (product + kv_bias).astype(jnp.bfloat16)
    new_rows = jnp.take(by_slot, every_source, axis=0)
    dest = cache_rows(lengths, block_table, total)
    flat = cache.reshape(cache.shape[0] * cache.shape[1], cache.shape[2])
    return flat.at[dest].set(new_rows).reshape(cache.shape)


def solution(mesh):
    placed = (
        P(("groups", "loop"), None),
        P(("groups", "loop")),
        P("groups"),
        P("groups"),
        P(),
        P(),
        P(None, "loop"),
        P("loop"),
        P("groups", None, "loop"),
    )
    return jax.shard_map(
        local, mesh=mesh, in_specs=placed, out_specs=P("groups", None, "loop"), check_vma=False
    )
```

```python
import jax
import jax.numpy as jnp
from jax import lax
from jax.experimental import pallas as pl
from jax.experimental.pallas import tpu as pltpu
from jax.sharding import PartitionSpec as P

PAGE = 16


def layer_norm(rows, ln_gain, ln_bias):
    values = rows.astype(jnp.float32)
    center = values - jnp.mean(values, axis=-1, keepdims=True)
    spread = jnp.mean(center * center, axis=-1, keepdims=True)
    return (center * lax.rsqrt(spread + 1e-05) * ln_gain + ln_bias).astype(jnp.bfloat16)


def cache_rows(lengths, block_table, total):
    ends = jnp.cumsum(lengths)
    token = jnp.arange(total, dtype=jnp.int32)
    passed = (token[:, None] >= ends[None, :]).astype(jnp.int32)
    session = jnp.sum(passed, axis=1)
    position = token - jnp.sum(passed * lengths[None, :], axis=1)
    per_session = block_table.shape[0] // lengths.shape[0]
    entry = session * per_session + position // PAGE
    table_ids = jnp.arange(block_table.shape[0], dtype=jnp.int32)
    page = jnp.sum(jnp.where(table_ids[None, :] == entry[:, None], block_table[None, :], 0), axis=1)
    return page * PAGE + position % PAGE


SEGS = 6
RING = 8
MESH = pl.DeviceIdType.MESH


def kernel(
    store, source, lengths, table, gain, bias, weight, kv_bias, cache, out,
    normed, packed, rows, held, extra, total, every, spread, pages, meta,
    to_right, to_left, to_twin, from_ring, from_twin,
    meta_right, meta_left, meta_twin, meta_ring, meta_from_twin,
    weight_sem, cache_sem, out_sem,
):
    count, width = store.shape
    main = width * 3 // 4
    seg_width, third = main // SEGS, width // 4
    half = SEGS // 2
    features = kv_bias.shape[1]
    slots = 2 * RING * 16
    pages_rows = pages.shape[0]

    me = lax.axis_index("loop")
    core, chip = lax.rem(me, 2), me // 2
    side = RING // 2
    place = chip // 2 + lax.rem(chip, 2) * (RING - 1 - 2 * (chip // 2))

    def device(step, which):
        at = lax.rem(place + step + RING, RING)
        column = at // side
        line = at + column * (RING - 1 - 2 * at)
        return 2 * (2 * line + column) + which

    right, left, twin = device(1, core), device(-1, core), device(0, 1 - core)

    parts = weight_sem.shape[0]
    depth = width // parts

    def weight_copy(i):
        span = pl.ds(pl.multiple_of(i * depth, depth), depth)
        return pltpu.make_async_copy(weight.at[span], held.at[span], weight_sem.at[i])

    barrier = pltpu.get_barrier_semaphore()
    for other in (right, left, twin):
        pl.semaphore_signal(barrier, inc=1, device_id={"loop": other}, device_id_type=MESH)
    for i in range(parts):
        weight_copy(i).start()
    cache_copy = pltpu.make_async_copy(cache, pages, cache_sem)
    cache_copy.start()

    values = store[...].astype(jnp.float32)
    center = values - jnp.mean(values, axis=-1, keepdims=True)
    var = jnp.mean(center * center, axis=-1, keepdims=True)
    normed[0:count, :] = center * lax.rsqrt(var + 1e-05) * gain[...] + bias[...]
    packed[0:count, :] = normed[0:count, 0:main]
    for s in range(3):
        packed[12:16, s * third:(s + 1) * third] = normed[4 * s:4 * s + 4, main:width]

    def row(m, which):
        return pl.multiple_of((2 * m + which) * 16, 16)

    rows[pl.ds(row(0, core), 16), :] = packed[...].astype(jnp.bfloat16)

    line = lax.broadcasted_iota(jnp.int32, (16, 128), 0)
    marks = jnp.full((16, 128), -1, jnp.int32)
    for i in range(count):
        marks = jnp.where(line == i, source[i], marks)

    def meta_at(dev):
        return meta.at[pl.ds(pl.multiple_of(dev * 16, 16), 16)]

    meta[pl.ds(pl.multiple_of(me * 16, 16), 16), :] = marks.astype(jnp.float32).astype(jnp.bfloat16)

    def block(m, seg):
        return rows.at[pl.ds(row(m, core), 16), pl.ds(pl.multiple_of(seg * seg_width, 128), seg_width)]

    def remote(src, dst, send, recv, dev):
        return pltpu.make_async_remote_copy(
            src_ref=src, dst_ref=dst, send_sem=send, recv_sem=recv,
            device_id={"loop": dev}, device_id_type=MESH,
        )

    def right_copy(k, seg):
        return remote(
            block(2 * k - 1 if k else 0, seg), block(2 * k + 1, seg),
            to_right.at[k, seg], from_ring.at[0, k, seg], right,
        )

    def left_copy(k, seg):
        return remote(
            block(2 * k, seg), block(2 * k + 2 if k < 3 else 7, seg),
            to_left.at[k, seg], from_ring.at[1, k, seg], left,
        )

    def twin_copy(m, seg):
        return remote(block(m, seg), block(m, seg), to_twin.at[m, seg], from_twin.at[m, seg], twin)

    def meta_copy(way, k, owner):
        sends = (meta_right, meta_left)[way]
        ref = meta_at(device(owner, core))
        return remote(ref, ref, sends.at[k], meta_ring.at[way, k], (right, left)[way])

    def meta_twin_copy(m, owner, which):
        ref = meta_at(device(owner, which))
        return remote(ref, ref, meta_twin.at[m], meta_from_twin.at[m], twin)

    pl.semaphore_wait(barrier, 3)

    @pl.loop(0, half)
    def _(j):
        right_copy(0, j).start()
        left_copy(0, j + half).start()

    meta_copy(0, 0, 0).start()
    meta_copy(1, 0, 0).start()
    meta_twin_copy(0, 0, core).start()

    @pl.loop(0, SEGS)
    def _(seg):
        twin_copy(0, seg).start()

    total[...] = jnp.zeros_like(total)
    extra[...] = jnp.zeros_like(extra)

    @pl.loop(0, half)
    def _(j):
        right_copy(0, j).wait_send()
        right_copy(0, j + half).start()
        left_copy(0, j + half).wait_send()
        left_copy(0, j).start()

    def multiply(base, size, seg):
        cols = pl.ds(pl.multiple_of(seg * seg_width, 128), seg_width)
        deep = pl.ds(pl.multiple_of(seg * seg_width, seg_width), seg_width)
        total[base:base + size, :] += jnp.dot(
            rows[base:base + size, cols], held[deep, :], preferred_element_type=jnp.float32
        )

    def collect(base, size, at):
        for b in range(size // 16):
            for s in range(3):
                piece = rows[base + 16 * b:base + 16 * b + 16, s * third:(s + 1) * third]
                spot = at + 16 * b + 4 * s
                extra[spot:spot + 4, :] = piece.astype(jnp.float32)[12:16]

    def finish(base, size, owners):
        result = total[base:base + size, :] + jnp.dot(
            extra[0:size, :].astype(jnp.bfloat16), held[main:width, :],
            preferred_element_type=jnp.float32,
        )
        result = (result + kv_bias[...]).astype(jnp.bfloat16)
        for b in range(size // 16):
            dev = device(owners[b // 2], b % 2)
            every[pl.ds(pl.multiple_of(dev * 16, 16), 16), :] = result[16 * b:16 * b + 16]

    def arrived(members, seg):
        for m in members:
            twin_copy(m, seg).wait_recv()

    for k in range(1, 4):
        meta_copy(0, k - 1, -k).wait_recv()
        meta_copy(0, k, -k).start()
        meta_twin_copy(2 * k - 1, -k, core).start()
        meta_copy(1, k - 1, k).wait_recv()
        if k < 3:
            meta_copy(1, k, k).start()
        meta_twin_copy(2 * k, k, core).start()
        for h in range(2):
            @pl.loop(0, half)
            def _(j, k=k, h=h):
                first, second = (j, j + half) if h == 0 else (j + half, j)
                right_copy(k - 1, first).wait_recv()
                if k < 3 or h == 0:
                    right_copy(k - 1 + h, second).wait_send()
                    right_copy(k, first).start()
                twin_copy(2 * k - 1, first).start()
                left_copy(k - 1, second).wait_recv()
                if k < 3 or h == 0:
                    left_copy(k - 1 + h, first).wait_send()
                    left_copy(k, second).start()
                twin_copy(2 * k, second).start()
                if k == 3:
                    arrived(range(5), first)
                    weight_copy(first).wait()
                    multiply(0, 160, first)

    meta_copy(0, 3, -4).wait_recv()
    meta_twin_copy(7, -4, core).start()

    for m, owner in ((0, 0), (1, -1), (2, 1), (3, -2), (4, 2), (5, -3), (6, 3), (7, -4)):
        meta_twin_copy(m, owner, 1 - core).wait_recv()
    slot = lax.broadcasted_iota(jnp.int32, (1, slots), 1)
    index = (slot // 16) * count + lax.rem(slot, 16)
    real = lax.rem(slot, 16) < count
    wanted = jnp.where(real, index, -2).astype(jnp.float32)
    asked = meta[...].astype(jnp.float32)
    asked = jnp.concatenate([asked] * (slots // 128), axis=1)
    pick = jnp.where(asked == wanted, 1.0, 0.0).astype(jnp.bfloat16)
    sessions, entries = lengths.shape[0], table.shape[0]
    session = jnp.zeros_like(index)
    position = index
    end = jnp.int32(0)
    for s in range(sessions):
        end = end + lengths[s]
        passed = index >= end
        session = session + jnp.where(passed, 1, 0)
        position = position - jnp.where(passed, lengths[s], 0)
    entry = session * (entries // sessions) + lax.shift_right_logical(position, 4)
    page = jnp.zeros_like(index)
    for e in range(entries):
        page = jnp.where(entry == e, table[e], page)
    dest = jnp.where(real, page * PAGE + jnp.bitwise_and(position, PAGE - 1), -1)
    where = lax.broadcasted_iota(jnp.int32, (pages_rows, slots), 0)
    put = jnp.where(where == dest, 1.0, 0.0).astype(jnp.bfloat16)
    spread[...] = jnp.dot(put, pick, preferred_element_type=jnp.float32).astype(jnp.bfloat16)
    cache_copy.wait()
    for i in range(SEGS, parts):
        weight_copy(i).wait()
    collect(0, 160, 0)
    finish(0, 160, (0, -1, 1, -2, 2))

    def pair(j):
        arrived((5, 6, 7), j)
        arrived((5, 6, 7), j + half)
        multiply(160, 96, j)
        multiply(160, 96, j + half)

    for j in range(half):
        right_copy(3, j).wait_recv()
        twin_copy(7, j).start()
        left_copy(3, j + half).wait_recv()
        twin_copy(7, j + half).start()
        if j > 0:
            pair(j - 1)
    pair(half - 1)
    collect(160, 96, 0)
    finish(160, 96, (-3, 3, -4))

    chunks = out_sem.shape[0]
    high = pages_rows // chunks

    def out_copy(i):
        span = pl.ds(pl.multiple_of(i * high, 16), high)
        return pltpu.make_async_copy(pages.at[span], out.at[span], out_sem.at[i])

    @pl.loop(0, chunks)
    def _(i):
        span = pl.ds(pl.multiple_of(i * high, 16), high)
        choice = spread[span, :]
        new = jnp.dot(choice, every[...], preferred_element_type=jnp.float32)
        taken = jnp.sum(choice.astype(jnp.float32), axis=1, keepdims=True) > 0.5
        pages[span, :] = jnp.where(taken, new, pages[span, :].astype(jnp.float32)).astype(jnp.bfloat16)
        out_copy(i).start()

    for k in range(4):
        meta_copy(0, k, -k).wait_send()
        if k < 3:
            meta_copy(1, k, k).wait_send()

    @pl.loop(0, half)
    def _(j):
        right_copy(3, j).wait_send()
        left_copy(3, j + half).wait_send()

    for m, owner in ((0, 0), (1, -1), (2, 1), (3, -2), (4, 2), (5, -3), (6, 3), (7, -4)):
        meta_twin_copy(m, owner, core).wait_send()

        @pl.loop(0, SEGS)
        def _(seg, m=m):
            twin_copy(m, seg).wait_send()

    @pl.loop(0, chunks)
    def _(i):
        out_copy(i).wait()


def fused(store, source, lengths, table, ln_gain, ln_bias, kv_weight, kv_bias, cache):
    count, width = store.shape
    features = kv_weight.shape[1]
    pages_rows = cache.shape[0] * cache.shape[1]
    slots = 2 * RING * 16
    parts, chunks = 8, 6
    vmem, smem, hbm = (
        pl.BlockSpec(memory_space=pltpu.VMEM),
        pl.BlockSpec(memory_space=pltpu.SMEM),
        pl.BlockSpec(memory_space=pltpu.HBM),
    )
    dma = pltpu.SemaphoreType.DMA
    result = pl.pallas_call(
        kernel,
        out_shape=jax.ShapeDtypeStruct((pages_rows, features), jnp.bfloat16),
        in_specs=[vmem, smem, smem, smem, vmem, vmem, hbm, vmem, hbm],
        out_specs=hbm,
        scratch_shapes=[
            pltpu.VMEM((16, width), jnp.float32),
            pltpu.VMEM((16, width * 3 // 4), jnp.float32),
            pltpu.VMEM((slots, width * 3 // 4), jnp.bfloat16),
            pltpu.VMEM((width, features), jnp.bfloat16),
            pltpu.VMEM((160, width // 4), jnp.float32),
            pltpu.VMEM((slots, features), jnp.float32),
            pltpu.VMEM((slots, features), jnp.bfloat16),
            pltpu.VMEM((pages_rows, slots), jnp.bfloat16),
            pltpu.VMEM((pages_rows, features), jnp.bfloat16),
            pltpu.VMEM((slots, 128), jnp.bfloat16),
            dma((4, SEGS)), dma((4, SEGS)), dma((8, SEGS)), dma((2, 4, SEGS)), dma((8, SEGS)),
            dma((4,)), dma((4,)), dma((8,)), dma((2, 4)), dma((8,)),
            dma((parts,)), dma, dma((chunks,)),
        ],
        compiler_params=pltpu.CompilerParams(
            collective_id=0, has_side_effects=True, vmem_limit_bytes=56 * 1024 * 1024
        ),
        cost_estimate=pl.CostEstimate(
            flops=2 * slots * width * features, transcendentals=0,
            bytes_accessed=2 * width * features + 4 * pages_rows * features,
        ),
    )(
        store, source, lengths, table, ln_gain.reshape(1, width), ln_bias.reshape(1, width),
        kv_weight, kv_bias.reshape(1, features), cache.reshape(pages_rows, features),
    )
    return result.reshape(cache.shape)


def local(store, source, lengths, block_table, ln_gain, ln_bias, kv_weight, kv_bias, cache):
    rows_dev = store.shape[0]
    devices = lax.axis_size("loop")
    total = rows_dev * devices
    if devices == 2 * RING and rows_dev == 12:
        return fused(store, source, lengths, block_table, ln_gain, ln_bias, kv_weight, kv_bias, cache)
    every_source = lax.all_gather(source, "loop", axis=0, tiled=True)
    product = jnp.dot(
        lax.all_gather(layer_norm(store, ln_gain, ln_bias), "loop", axis=0, tiled=True),
        kv_weight,
        preferred_element_type=jnp.float32,
    )
    by_slot = (product + kv_bias).astype(jnp.bfloat16)
    new_rows = jnp.take(by_slot, every_source, axis=0)
    dest = cache_rows(lengths, block_table, total)
    flat = cache.reshape(cache.shape[0] * cache.shape[1], cache.shape[2])
    return flat.at[dest].set(new_rows).reshape(cache.shape)


def solution(mesh):
    placed = (
        P(("groups", "loop"), None),
        P(("groups", "loop")),
        P("groups"),
        P("groups"),
        P(),
        P(),
        P(None, "loop"),
        P("loop"),
        P("groups", None, "loop"),
    )
    return jax.shard_map(
        local, mesh=mesh, in_specs=placed, out_specs=P("groups", None, "loop"), check_vma=False
    )
```

```python
import jax
import jax.numpy as jnp
from jax import lax
from jax.experimental import pallas as pl
from jax.experimental.pallas import tpu as pltpu
from jax.sharding import PartitionSpec as P

PAGE = 16


def layer_norm(rows, ln_gain, ln_bias):
    values = rows.astype(jnp.float32)
    center = values - jnp.mean(values, axis=-1, keepdims=True)
    spread = jnp.mean(center * center, axis=-1, keepdims=True)
    return (center * lax.rsqrt(spread + 1e-05) * ln_gain + ln_bias).astype(jnp.bfloat16)


def cache_rows(lengths, block_table, total):
    ends = jnp.cumsum(lengths)
    token = jnp.arange(total, dtype=jnp.int32)
    passed = (token[:, None] >= ends[None, :]).astype(jnp.int32)
    session = jnp.sum(passed, axis=1)
    position = token - jnp.sum(passed * lengths[None, :], axis=1)
    per_session = block_table.shape[0] // lengths.shape[0]
    entry = session * per_session + position // PAGE
    table_ids = jnp.arange(block_table.shape[0], dtype=jnp.int32)
    page = jnp.sum(jnp.where(table_ids[None, :] == entry[:, None], block_table[None, :], 0), axis=1)
    return page * PAGE + position % PAGE


SEGS = 6
RING = 8
MESH = pl.DeviceIdType.MESH


def kernel(
    store, source, lengths, table, gain, bias, weight, kv_bias, cache, out,
    normed, packed, rows, held, extra, total, every, spread, pages, meta,
    to_right, to_left, to_twin, from_ring, from_twin,
    meta_right, meta_left, meta_twin, meta_ring, meta_from_twin,
    weight_sem, cache_sem, out_sem,
):
    count, width = store.shape
    main = width * 3 // 4
    seg_width, third = main // SEGS, width // 4
    half = SEGS // 2
    features = kv_bias.shape[1]
    slots = 2 * RING * 16
    pages_rows = pages.shape[0]

    me = lax.axis_index("loop")
    core, chip = lax.rem(me, 2), me // 2
    side = RING // 2
    place = chip // 2 + lax.rem(chip, 2) * (RING - 1 - 2 * (chip // 2))

    def device(step, which):
        at = lax.rem(place + step + RING, RING)
        column = at // side
        line = at + column * (RING - 1 - 2 * at)
        return 2 * (2 * line + column) + which

    right, left, twin = device(1, core), device(-1, core), device(0, 1 - core)

    parts = weight_sem.shape[0]
    depth = width // parts

    def weight_copy(i):
        span = pl.ds(pl.multiple_of(i * depth, depth), depth)
        return pltpu.make_async_copy(weight.at[span], held.at[span], weight_sem.at[i])

    barrier = pltpu.get_barrier_semaphore()
    for other in (right, left, twin):
        pl.semaphore_signal(barrier, inc=1, device_id={"loop": other}, device_id_type=MESH)
    for i in range(parts):
        weight_copy(i).start()
    cache_copy = pltpu.make_async_copy(cache, pages, cache_sem)
    cache_copy.start()

    values = store[...].astype(jnp.float32)
    center = values - jnp.mean(values, axis=-1, keepdims=True)
    var = jnp.mean(center * center, axis=-1, keepdims=True)
    normed[0:count, :] = center * lax.rsqrt(var + 1e-05) * gain[...] + bias[...]
    packed[0:count, :] = normed[0:count, 0:main]
    for s in range(3):
        packed[12:16, s * third:(s + 1) * third] = normed[4 * s:4 * s + 4, main:width]

    def row(m, which):
        return pl.multiple_of((2 * m + which) * 16, 16)

    rows[pl.ds(row(0, core), 16), :] = packed[...].astype(jnp.bfloat16)

    line = lax.broadcasted_iota(jnp.int32, (16, 128), 0)
    marks = jnp.full((16, 128), -1, jnp.int32)
    for i in range(count):
        marks = jnp.where(line == i, source[i], marks)

    def meta_at(dev):
        return meta.at[pl.ds(pl.multiple_of(dev * 16, 16), 16)]

    meta[pl.ds(pl.multiple_of(me * 16, 16), 16), :] = marks.astype(jnp.float32).astype(jnp.bfloat16)

    def block(m, seg):
        return rows.at[pl.ds(row(m, core), 16), pl.ds(pl.multiple_of(seg * seg_width, 128), seg_width)]

    def remote(src, dst, send, recv, dev):
        return pltpu.make_async_remote_copy(
            src_ref=src, dst_ref=dst, send_sem=send, recv_sem=recv,
            device_id={"loop": dev}, device_id_type=MESH,
        )

    def right_copy(k, seg):
        return remote(
            block(2 * k - 1 if k else 0, seg), block(2 * k + 1, seg),
            to_right.at[k, seg], from_ring.at[0, k, seg], right,
        )

    def left_copy(k, seg):
        return remote(
            block(2 * k, seg), block(2 * k + 2 if k < 3 else 7, seg),
            to_left.at[k, seg], from_ring.at[1, k, seg], left,
        )

    def twin_copy(m, seg):
        return remote(block(m, seg), block(m, seg), to_twin.at[m, seg], from_twin.at[m, seg], twin)

    def meta_copy(way, k, owner):
        sends = (meta_right, meta_left)[way]
        ref = meta_at(device(owner, core))
        return remote(ref, ref, sends.at[k], meta_ring.at[way, k], (right, left)[way])

    def meta_twin_copy(m, owner, which):
        ref = meta_at(device(owner, which))
        return remote(ref, ref, meta_twin.at[m], meta_from_twin.at[m], twin)

    pl.semaphore_wait(barrier, 3)

    @pl.loop(0, half)
    def _(j):
        right_copy(0, j).start()
        left_copy(0, j + half).start()

    meta_copy(0, 0, 0).start()
    meta_copy(1, 0, 0).start()
    meta_twin_copy(0, 0, core).start()

    @pl.loop(0, SEGS)
    def _(seg):
        twin_copy(0, seg).start()

    total[...] = jnp.zeros_like(total)
    extra[...] = jnp.zeros_like(extra)

    @pl.loop(0, half)
    def _(j):
        right_copy(0, j).wait_send()
        right_copy(0, j + half).start()
        left_copy(0, j + half).wait_send()
        left_copy(0, j).start()

    def multiply(base, size, seg):
        cols = pl.ds(pl.multiple_of(seg * seg_width, 128), seg_width)
        deep = pl.ds(pl.multiple_of(seg * seg_width, seg_width), seg_width)
        total[base:base + size, :] += jnp.dot(
            rows[base:base + size, cols], held[deep, :], preferred_element_type=jnp.float32
        )

    def collect(base, size, at):
        for b in range(size // 16):
            for s in range(3):
                piece = rows[base + 16 * b:base + 16 * b + 16, s * third:(s + 1) * third]
                spot = at + 16 * b + 4 * s
                extra[spot:spot + 4, :] = piece.astype(jnp.float32)[12:16]

    def finish(base, size, owners):
        result = total[base:base + size, :] + jnp.dot(
            extra[0:size, :].astype(jnp.bfloat16), held[main:width, :],
            preferred_element_type=jnp.float32,
        )
        result = (result + kv_bias[...]).astype(jnp.bfloat16)
        for b in range(size // 16):
            dev = device(owners[b // 2], b % 2)
            every[pl.ds(pl.multiple_of(dev * 16, 16), 16), :] = result[16 * b:16 * b + 16]

    def arrived(members, seg):
        for m in members:
            twin_copy(m, seg).wait_recv()

    for k in range(1, 4):
        meta_copy(0, k - 1, -k).wait_recv()
        meta_copy(0, k, -k).start()
        meta_twin_copy(2 * k - 1, -k, core).start()
        meta_copy(1, k - 1, k).wait_recv()
        if k < 3:
            meta_copy(1, k, k).start()
        meta_twin_copy(2 * k, k, core).start()
        for h in range(2):
            @pl.loop(0, half)
            def _(j, k=k, h=h):
                first, second = (j, j + half) if h == 0 else (j + half, j)
                right_copy(k - 1, first).wait_recv()
                if k < 3 or h == 0:
                    right_copy(k - 1 + h, second).wait_send()
                    right_copy(k, first).start()
                twin_copy(2 * k - 1, first).start()
                left_copy(k - 1, second).wait_recv()
                if k < 3 or h == 0:
                    left_copy(k - 1 + h, first).wait_send()
                    left_copy(k, second).start()
                twin_copy(2 * k, second).start()
                if k == 3:
                    arrived(range(5), first)
                    weight_copy(first).wait()
                    multiply(0, 160, first)

    meta_copy(0, 3, -4).wait_recv()
    meta_twin_copy(7, -4, core).start()

    for m, owner in ((0, 0), (1, -1), (2, 1), (3, -2), (4, 2), (5, -3), (6, 3), (7, -4)):
        meta_twin_copy(m, owner, 1 - core).wait_recv()
    slot = lax.broadcasted_iota(jnp.int32, (1, slots), 1)
    index = (slot // 16) * count + lax.rem(slot, 16)
    real = lax.rem(slot, 16) < count
    wanted = jnp.where(real, index, -2).astype(jnp.float32)
    asked = meta[...].astype(jnp.float32)
    asked = jnp.concatenate([asked] * (slots // 128), axis=1)
    pick = jnp.where(asked == wanted, 1.0, 0.0).astype(jnp.bfloat16)
    sessions, entries = lengths.shape[0], table.shape[0]
    session = jnp.zeros_like(index)
    position = index
    end = jnp.int32(0)
    for s in range(sessions):
        end = end + lengths[s]
        passed = index >= end
        session = session + jnp.where(passed, 1, 0)
        position = position - jnp.where(passed, lengths[s], 0)
    entry = session * (entries // sessions) + lax.shift_right_logical(position, 4)
    page = jnp.zeros_like(index)
    for e in range(entries):
        page = jnp.where(entry == e, table[e], page)
    dest = jnp.where(real, page * PAGE + jnp.bitwise_and(position, PAGE - 1), -1)
    where = lax.broadcasted_iota(jnp.int32, (pages_rows, slots), 0)
    put = jnp.where(where == dest, 1.0, 0.0).astype(jnp.bfloat16)
    spread[...] = jnp.dot(put, pick, preferred_element_type=jnp.float32).astype(jnp.bfloat16)
    cache_copy.wait()
    for i in range(SEGS, parts):
        weight_copy(i).wait()
    collect(0, 160, 0)
    finish(0, 160, (0, -1, 1, -2, 2))

    def pair(j):
        arrived((5, 6, 7), j)
        arrived((5, 6, 7), j + half)
        multiply(160, 96, j)
        multiply(160, 96, j + half)

    for j in range(half):
        right_copy(3, j).wait_recv()
        twin_copy(7, j).start()
        left_copy(3, j + half).wait_recv()
        twin_copy(7, j + half).start()
        if j > 0:
            pair(j - 1)
    arrived((5, 6), half - 1)
    arrived((5, 6), SEGS - 1)
    collect(160, 64, 0)
    arrived((7,), half - 1)
    arrived((7,), SEGS - 1)
    collect(224, 32, 64)
    multiply(160, 96, half - 1)
    multiply(160, 96, SEGS - 1)
    finish(160, 96, (-3, 3, -4))

    chunks = out_sem.shape[0]
    high = pages_rows // chunks

    def out_copy(i):
        span = pl.ds(pl.multiple_of(i * high, 16), high)
        return pltpu.make_async_copy(pages.at[span], out.at[span], out_sem.at[i])

    @pl.loop(0, chunks)
    def _(i):
        span = pl.ds(pl.multiple_of(i * high, 16), high)
        choice = spread[span, :]
        new = jnp.dot(choice, every[...], preferred_element_type=jnp.float32)
        taken = jnp.sum(choice.astype(jnp.float32), axis=1, keepdims=True) > 0.5
        pages[span, :] = jnp.where(taken, new, pages[span, :].astype(jnp.float32)).astype(jnp.bfloat16)
        out_copy(i).start()

    for k in range(4):
        meta_copy(0, k, -k).wait_send()
        if k < 3:
            meta_copy(1, k, k).wait_send()

    @pl.loop(0, half)
    def _(j):
        right_copy(3, j).wait_send()
        left_copy(3, j + half).wait_send()

    for m, owner in ((0, 0), (1, -1), (2, 1), (3, -2), (4, 2), (5, -3), (6, 3), (7, -4)):
        meta_twin_copy(m, owner, core).wait_send()

        @pl.loop(0, SEGS)
        def _(seg, m=m):
            twin_copy(m, seg).wait_send()

    @pl.loop(0, chunks)
    def _(i):
        out_copy(i).wait()


def fused(store, source, lengths, table, ln_gain, ln_bias, kv_weight, kv_bias, cache):
    count, width = store.shape
    features = kv_weight.shape[1]
    pages_rows = cache.shape[0] * cache.shape[1]
    slots = 2 * RING * 16
    parts, chunks = 8, 3
    vmem, smem, hbm = (
        pl.BlockSpec(memory_space=pltpu.VMEM),
        pl.BlockSpec(memory_space=pltpu.SMEM),
        pl.BlockSpec(memory_space=pltpu.HBM),
    )
    dma = pltpu.SemaphoreType.DMA
    result = pl.pallas_call(
        kernel,
        out_shape=jax.ShapeDtypeStruct((pages_rows, features), jnp.bfloat16),
        in_specs=[vmem, smem, smem, smem, vmem, vmem, hbm, vmem, hbm],
        out_specs=hbm,
        scratch_shapes=[
            pltpu.VMEM((16, width), jnp.float32),
            pltpu.VMEM((16, width * 3 // 4), jnp.float32),
            pltpu.VMEM((slots, width * 3 // 4), jnp.bfloat16),
            pltpu.VMEM((width, features), jnp.bfloat16),
            pltpu.VMEM((160, width // 4), jnp.float32),
            pltpu.VMEM((slots, features), jnp.float32),
            pltpu.VMEM((slots, features), jnp.bfloat16),
            pltpu.VMEM((pages_rows, slots), jnp.bfloat16),
            pltpu.VMEM((pages_rows, features), jnp.bfloat16),
            pltpu.VMEM((slots, 128), jnp.bfloat16),
            dma((4, SEGS)), dma((4, SEGS)), dma((8, SEGS)), dma((2, 4, SEGS)), dma((8, SEGS)),
            dma((4,)), dma((4,)), dma((8,)), dma((2, 4)), dma((8,)),
            dma((parts,)), dma, dma((chunks,)),
        ],
        compiler_params=pltpu.CompilerParams(
            collective_id=0, has_side_effects=True, vmem_limit_bytes=56 * 1024 * 1024
        ),
        cost_estimate=pl.CostEstimate(
            flops=2 * slots * width * features, transcendentals=0,
            bytes_accessed=2 * width * features + 4 * pages_rows * features,
        ),
    )(
        store, source, lengths, table, ln_gain.reshape(1, width), ln_bias.reshape(1, width),
        kv_weight, kv_bias.reshape(1, features), cache.reshape(pages_rows, features),
    )
    return result.reshape(cache.shape)


def local(store, source, lengths, block_table, ln_gain, ln_bias, kv_weight, kv_bias, cache):
    rows_dev = store.shape[0]
    devices = lax.axis_size("loop")
    total = rows_dev * devices
    if devices == 2 * RING and rows_dev == 12:
        return fused(store, source, lengths, block_table, ln_gain, ln_bias, kv_weight, kv_bias, cache)
    every_source = lax.all_gather(source, "loop", axis=0, tiled=True)
    product = jnp.dot(
        lax.all_gather(layer_norm(store, ln_gain, ln_bias), "loop", axis=0, tiled=True),
        kv_weight,
        preferred_element_type=jnp.float32,
    )
    by_slot = (product + kv_bias).astype(jnp.bfloat16)
    new_rows = jnp.take(by_slot, every_source, axis=0)
    dest = cache_rows(lengths, block_table, total)
    flat = cache.reshape(cache.shape[0] * cache.shape[1], cache.shape[2])
    return flat.at[dest].set(new_rows).reshape(cache.shape)


def solution(mesh):
    placed = (
        P(("groups", "loop"), None),
        P(("groups", "loop")),
        P("groups"),
        P("groups"),
        P(),
        P(),
        P(None, "loop"),
        P("loop"),
        P("groups", None, "loop"),
    )
    return jax.shard_map(
        local, mesh=mesh, in_specs=placed, out_specs=P("groups", None, "loop"), check_vma=False
    )
```
